256 devices in a mesh: date: 8 (over x, y_hi), rng: 32 (over z, y_lo, core).
Axes of the slice: x: 4, y: 4 (y_hi: 2, y_lo: 2; y = y_hi * 2 + y_lo), z: 8, core: 2. Of those that a mesh axis runs over, the one named last changes fastest.
Arguments:
- slc: bfloat16 [2, 32, 256, 16384], P(None, 'date', None, 'rng'), may hold values from -6 to 6
- shift_table: int32 [32, 16384], P('date', 'rng'), may hold values from -189 to 188
- phase_table: int32 [32, 16384], P('date', 'rng'), may hold values from 0 to 255
- reference_ids: int32 [2], replicated, may hold values from 0 to 31
Outputs:
- multilook: float32 [2, 32, 64, 1024], P(None, 'date', None, 'rng')
- coherence: float32 [32, 64, 1024], P('date', None, 'rng')
The draws below stay inside these ranges and needn't reach their ends.
All inputs are finite; a program needn't handle non-finite values.
Results may differ from the reference program's by a relative error of at most 0.0041.
Values may be sent and summed in bfloat16 or wider, within the bound.
A program may use at most 128 MiB of HBM per device.

```python
import jax
import jax.numpy as jnp
from jax import lax

AZ = 256
HALO = 192
TAPS = 8
PHASES = 256
LOOK_AZ = 4
LOOK_RG = 16
DATES = 32
NR = 16384
MINI_DATES = 16
MINI_STACKS = 2


def draw_shift_table(key, part):
    key = jax.random.fold_in(key, 11)
    first_key, second_key = jax.random.split(key)
    shifts = jax.random.randint(first_key, (DATES, NR), 3 - HALO, HALO - 3, dtype=jnp.int32)
    positions = jax.random.randint(second_key, (DATES,), 0, NR - 1, dtype=jnp.int32)
    date_rows = jnp.arange(DATES, dtype=jnp.int32)
    shifts = shifts.at[date_rows, positions].set(3 - HALO)
    shifts = shifts.at[date_rows, positions + 1].set(HALO - 4)
    return shifts


def plant(result, stream_key, smallest, high):
    spot = [jax.random.randint(jax.random.fold_in(stream_key, axis), (), 0, length) for axis, length in enumerate(result.shape)]
    widest = result.shape.index(max(result.shape))
    next_to = spot[:widest] + [(spot[widest] + 1) % result.shape[widest]] + spot[widest + 1:]
    return result.at[tuple(spot)].set(smallest).at[tuple(next_to)].set(high)


def block_scale(own_key, extent, pieces, smallest, largest):
    def one(axis_at, blocks):
        heights = jax.random.uniform(jax.random.fold_in(jax.random.fold_in(own_key, 6), axis_at), (blocks,), jnp.float32, smallest / len(pieces), largest / len(pieces))
        return jnp.repeat(jnp.exp(heights), extent[axis_at] // blocks).reshape((-1,) + (1,) * (len(extent) - axis_at - 1))

    gain = one(*pieces[0])
    for cut in pieces[1:]:
        gain = gain * one(*cut)
    return gain


def bell_draw(key, shape, scale, reach, shards=(), kind=jnp.bfloat16):
    values = jax.random.normal(key, shape, jnp.float32) * scale
    if len(shards) > 0:
        values = block_scale(key, shape, shards, -0.22, 0.18) * values
    return jnp.clip(values, min=-reach, max=reach).astype(kind)


def setup_inputs(seed: int = 0) -> dict:
    streams_of = jax.random.split(jax.random.key(seed), 5)
    return {
        "slc": bell_draw(streams_of[0], (2, DATES, AZ, NR), 1.0, 6.0, ((1, 8), (3, 32))),
        "shift_table": draw_shift_table(jax.random.fold_in(streams_of[4], 71), 0),
        "phase_table": plant(jax.random.randint(streams_of[2], (DATES, NR), 0, PHASES), jax.random.fold_in(streams_of[2], 1), 0, PHASES - 1).astype(jnp.int32),
        "reference_ids": jax.random.randint(streams_of[3], (MINI_STACKS,), 0, DATES).astype(jnp.int32),
    }


def kernel_table():
    fraction = jnp.arange(PHASES, dtype=jnp.float32) / PHASES
    tap_offset = jnp.arange(TAPS, dtype=jnp.float32) - (TAPS // 2 - 1)
    distance = tap_offset[:, None] - fraction[None, :]
    weight = jnp.sinc(distance) * (0.5 + 0.5 * jnp.cos(jnp.pi * distance / (TAPS // 2 + 1)))
    return weight / lax.optimization_barrier(jnp.sum(weight, axis=0, keepdims=True))

def resample_date(padded, shifts, phases, kernel):
    columns = shifts.shape[0]
    onehot = (phases[None, :] == jnp.arange(PHASES, dtype=jnp.int32)[:, None]).astype(jnp.float32)
    coefficients = jnp.dot(kernel, onehot, precision=lax.Precision.HIGHEST)
    first_tap = jnp.arange(columns, dtype=jnp.int32) + shifts + (HALO - TAPS // 2 + 1)
    summed = jnp.zeros(padded.shape[:-1] + (columns,), jnp.float32)
    for k in range(TAPS):
        picked = jnp.take(padded, (first_tap + k).astype(jnp.int32), axis=-1)
        summed = summed + coefficients[k] * picked.astype(jnp.float32)
    return summed.astype(jnp.bfloat16)

def patch_sum(v):
    n, lines, pixels = v.shape
    return v.reshape(n, lines // LOOK_AZ, LOOK_AZ, pixels // LOOK_RG, LOOK_RG).sum(axis=(2, 4))

def patch_stats(dates, ref_tile):
    date_re = dates[0].astype(jnp.float32)
    date_im = dates[1].astype(jnp.float32)
    ref_re = ref_tile[0].astype(jnp.float32)[None]
    ref_im = ref_tile[1].astype(jnp.float32)[None]
    ifg_re = date_re * ref_re + date_im * ref_im
    ifg_im = date_im * ref_re - date_re * ref_im
    power_a = date_re * date_re + date_im * date_im
    power_b = ref_re * ref_re + ref_im * ref_im
    sum_re = patch_sum(ifg_re)
    sum_im = patch_sum(ifg_im)
    sum_a = patch_sum(power_a)
    sum_b = patch_sum(power_b)
    multilook = jnp.stack([sum_re, sum_im]) / (LOOK_AZ * LOOK_RG)
    coherence = jnp.sqrt(sum_re * sum_re + sum_im * sum_im) / jnp.sqrt(sum_a * sum_b + 1e-06)
    return (multilook, coherence)

def reference(slc, shift_table, phase_table, reference_ids):
    kernel = kernel_table()
    padded = jnp.pad(slc, ((0, 0), (0, 0), (0, 0), (HALO, HALO)))

    def one_date(d):
        return resample_date(padded[:, d], shift_table[d], phase_table[d], kernel)
    resampled = lax.map(one_date, jnp.arange(DATES, dtype=jnp.int32))

    def one_look(d):
        ref_tile = resampled[reference_ids[d // MINI_DATES]]
        multilook, coherence = patch_stats(resampled[d][:, None], ref_tile)
        return (multilook[:, 0], coherence[0])
    multilook, coherence = lax.map(one_look, jnp.arange(DATES, dtype=jnp.int32))
    return (jnp.transpose(multilook, (1, 0, 2, 3)), coherence)
```

```python
import functools

import jax
import jax.numpy as jnp
import numpy as np
from jax import lax
from jax.experimental import pallas as pl
from jax.experimental.pallas import tpu as pltpu
from jax.sharding import PartitionSpec as P

TAPS = 8
PHASES = 256
LOOK_AZ = 4
LOOK_RG = 16
CHUNKS = 4
WIN = 768
MESH = pl.DeviceIdType.MESH
BF16 = jnp.bfloat16
F32 = jnp.float32


def tap_table():
    fraction = np.arange(PHASES) / PHASES
    tap_offset = np.arange(TAPS) - (TAPS // 2 - 1)
    t = tap_offset[:, None] - fraction[None, :]
    weight = np.sinc(t) * (0.5 + 0.5 * np.cos(np.pi * t / (TAPS // 2 + 1)))
    weight = jnp.asarray(weight / weight.sum(axis=0, keepdims=True), F32)
    high = weight.astype(BF16)
    low = (weight - high.astype(F32)).astype(BF16)
    return jnp.concatenate([high, low], axis=0)


def half_turn(v):
    return pltpu.roll(v.astype(F32), 64, 1).astype(BF16)


def two_rows(v):
    return v.reshape(-1, v.shape[-1])


def kernel(
    dates, rngs, chunks, half_lines,
    ids, shift_ref, phase_ref, table_ref, slc_hbm,
    ml_ref, coh_ref,
    own, near_send, far_send, near_recv, far_recv, band_hi, band_lo,
    resampled, outer_in, outer_sel, inner_in, inner_sel, cross_in, final_own, final_in,
    lane_sums, looks,
    own_sem, halo_send, halo_recv, ref_send, ref_recv,
):
    rows = half_lines // chunks
    me_d, me_r = lax.axis_index("date"), lax.axis_index("rng")
    x, yh = me_d // 2, me_d % 2
    outer_x = 3 - x
    inner_x = x + 1 - 2 * (x % 2)
    half = x % 2
    left, right = (me_r + rngs - 1) % rngs, (me_r + 1) % rngs
    stack = x // 2
    dev_outer = (outer_x * 2 + yh, me_r)
    dev_inner = (inner_x * 2 + yh, me_r)
    dev_cross = (x * 2 + 1 - yh, me_r)
    dev_left, dev_right = (me_d, left), (me_d, right)

    load = pltpu.make_async_copy(slc_hbm, own, own_sem)
    load.start()
    barrier = pltpu.get_barrier_semaphore()
    for device in (dev_left, dev_right, dev_outer, dev_inner, dev_cross):
        pl.semaphore_signal(barrier, inc=1, device_id=device, device_id_type=MESH)

    mine = jnp.where(stack == 0, ids[0], ids[1])
    other = jnp.where(stack == 0, ids[1], ids[0])
    slot_m, slot_o = mine % 4, other % 4
    p0 = slot_o
    same = slot_m == slot_o
    p1 = jnp.where(same, (slot_o + 1) % 4, slot_m)
    p2 = jnp.where((p0 != 0) & (p1 != 0), 0, jnp.where((p0 != 1) & (p1 != 1), 1, 2))
    p3 = 6 - p0 - p1 - p2
    order = (p0, p1, p2, p3)
    mine_at = jnp.where(same, 0, 1)
    owner = mine // 4
    owner_x, owner_yh = owner // 2, owner % 2

    lane = lax.broadcasted_iota(jnp.int32, (1, 128), 1)

    def stage(i):
        for re_im in range(2):
            near_send[0, i, re_im] = own[re_im, order[i], :, :, 384:512]
            near_send[1, i, re_im] = own[re_im, order[i], :, :, 0:128]
        for h in range(2):
            re = own[0, order[i], h, :, 256:384].astype(F32)
            im = own[1, order[i], h, :, 256:384].astype(F32)
            far_send[0, i, h] = jnp.where(lane < 64, pltpu.roll(re, 64, 1), im).astype(BF16)
            re = own[0, order[i], h, :, 128:256].astype(F32)
            im = own[1, order[i], h, :, 128:256].astype(F32)
            far_send[1, i, h] = jnp.where(lane < 64, re, pltpu.roll(im, 64, 1)).astype(BF16)

    def halo(group, j):
        at = pl.ds(j * rows, rows)
        pair = pl.ds(2 * group, 2)
        copies = []
        for side, device in enumerate((dev_right, dev_left)):
            copies.append(pltpu.make_async_remote_copy(
                src_ref=near_send.at[side, pair, :, :, at, :],
                dst_ref=near_recv.at[side, pair, :, :, at, :],
                send_sem=halo_send.at[group, j, side, 0],
                recv_sem=halo_recv.at[group, j, side, 0],
                device_id=device, device_id_type=MESH))
            copies.append(pltpu.make_async_remote_copy(
                src_ref=far_send.at[side, pair, :, at, :],
                dst_ref=far_recv.at[side, pair, :, at, :],
                send_sem=halo_send.at[group, j, side, 1],
                recv_sem=halo_recv.at[group, j, side, 1],
                device_id=device, device_id_type=MESH))
        return copies

    def step_copy(step, j):
        at = pl.ds(j * rows, rows)
        src, dst, device = (
            (resampled.at[0, :, :, at, :], outer_in.at[:, :, at, :], dev_outer),
            (outer_sel.at[:, 1 - half, at, :], inner_in.at[:, at, :], dev_inner),
            (inner_sel.at[:, at, :], cross_in.at[:, at, :], dev_cross),
            (final_own.at[:, at, :], final_in.at[:, at, :], dev_inner),
        )[step]
        return pltpu.make_async_remote_copy(
            src_ref=src, dst_ref=dst,
            send_sem=ref_send.at[step, j], recv_sem=ref_recv.at[step, j],
            device_id=device, device_id_type=MESH)

    def build_band(i):
        phase = phase_ref[order[i]]
        shift = shift_ref[order[i]]
        hot = jnp.where(
            lax.broadcasted_iota(jnp.int32, (PHASES, 512), 0) == phase, 1.0, 0.0).astype(BF16)
        taps = jnp.dot(table_ref[...], hot, preferred_element_type=F32)
        column = lax.broadcasted_iota(jnp.int32, (1, 512), 1)
        first = (column & 255) + shift + 253
        block = first >> 3
        place = lax.broadcasted_iota(jnp.int32, (8, 512), 0) - (first & 7)
        parts = []
        for base in (0, 8):
            now = jnp.zeros((8, 512), F32)
            later = jnp.zeros((8, 512), F32)
            for k in range(TAPS):
                tap = taps[base + k:base + k + 1, :]
                now = jnp.where(place == k, tap, now)
                if k > 0:
                    later = jnp.where(place + 8 == k, tap, later)
            parts.append((now, later))
        outside_left = (column < 256) & (me_r == 0)
        outside_right = (column >= 256) & (me_r == rngs - 1)
        regions = (jnp.where(outside_left, -9, block), block, jnp.where(outside_right, -9, block))
        for region, where_at in enumerate(regions):
            spread = jnp.broadcast_to(where_at, (8, 512))

            def fill(t, carry):
                masks = [spread == 2 * t + u for u in (-1, 0, 1)]
                for (now, later), band in zip(parts, (band_hi, band_lo)):
                    low = jnp.where(masks[1], now, jnp.where(masks[0], later, 0.0))
                    up = jnp.where(masks[2], now, jnp.where(masks[1], later, 0.0))
                    band[i, pl.ds(pl.multiple_of(t * 16, 16), 16), :] = (
                        jnp.concatenate([low, up], axis=0).astype(BF16))
                return carry

            lax.fori_loop(region * 16, region * 16 + 16, fill, 0)

    def resample(i, j):
        at = pl.ds(j * rows, rows)
        centre = two_rows(own[:, order[i], :, at, :])
        near = [two_rows(near_recv[side, i, :, :, at, :]) for side in range(2)]
        packed = [two_rows(far_recv[side, i, :, at, :]) for side in range(2)]
        before = jnp.concatenate([half_turn(packed[0]), packed[0]], axis=0)
        after = jnp.concatenate([packed[1], half_turn(packed[1])], axis=0)
        windows = (
            jnp.concatenate([before, near[0], centre], axis=1),
            jnp.concatenate([centre, near[1], after], axis=1),
        )
        for n, window in enumerate(windows):
            cols = pl.ds(n * 256, 256)
            total = jnp.dot(window, band_hi[i, :, cols], preferred_element_type=F32)
            total += jnp.dot(window, band_lo[i, :, cols], preferred_element_type=F32)
            resampled[i, :, :, at, cols] = total.astype(BF16).reshape(2, 2, rows, 256)

    def looks_of(j):
        at = pl.ds(j * rows, rows)
        group = lax.broadcasted_iota(jnp.int32, (512, 128), 0) // LOOK_RG
        ones = jnp.where(group == lax.broadcasted_iota(jnp.int32, (512, 128), 1), 1.0, 0.0).astype(BF16)

        def summed(v, row):
            high = v.astype(BF16)
            low = (v - high.astype(F32)).astype(BF16)
            lane_sums[row * rows:(row + 1) * rows, :] = (
                jnp.dot(high, ones, preferred_element_type=F32)
                + jnp.dot(low, ones, preferred_element_type=F32))

        out_rows = rows // LOOK_AZ
        for which, b_ref in ((half, final_own), (1 - half, final_in)):
            b_re, b_im = b_ref[0, at, :].astype(F32), b_ref[1, at, :].astype(F32)
            summed(b_re * b_re + b_im * b_im, 12)
            for i in range(4):
                a_re = resampled[i, 0, which, at, :].astype(F32)
                a_im = resampled[i, 1, which, at, :].astype(F32)
                summed(a_re * b_re + a_im * b_im, 3 * i)
                summed(a_im * b_re - a_re * b_im, 3 * i + 1)
                summed(a_re * a_re + a_im * a_im, 3 * i + 2)
            patches = sum(
                lane_sums[pl.ds(k, 13 * out_rows, stride=LOOK_AZ), :] for k in range(LOOK_AZ))
            sum_b = patches[12 * out_rows:13 * out_rows]
            to = pl.ds(j * out_rows, out_rows)
            for i in range(4):
                s_re, s_im, s_a = (
                    patches[(3 * i + u) * out_rows:(3 * i + u + 1) * out_rows] for u in range(3))
                looks[i, 0, which, to, :] = s_re / (LOOK_AZ * LOOK_RG)
                looks[i, 1, which, to, :] = s_im / (LOOK_AZ * LOOK_RG)
                looks[i, 2, which, to, :] = (
                    jnp.sqrt(s_re * s_re + s_im * s_im) / jnp.sqrt(s_a * sum_b + 1e-06))

    load.wait()
    stage(0)
    stage(1)
    pl.semaphore_wait(barrier, 5)
    started = []
    for j in range(chunks):
        for copy in halo(0, j):
            copy.start()
            started.append(copy)
    build_band(0)
    build_band(1)
    stage(2)
    stage(3)

    for t in range(chunks + 4):
        if t < chunks:
            for copy in halo(0, t):
                copy.wait_recv()
            resample(0, t)
            copy = step_copy(0, t)
            copy.start()
            started.append(copy)
            resample(1, t)
        if t == 0:
            for j in range(chunks):
                for copy in halo(1, j):
                    copy.start()
                    started.append(copy)
        if 0 <= t - 1 < chunks:
            j = t - 1
            at = pl.ds(j * rows, rows)
            step_copy(0, j).wait_recv()
            outer_sel[:, :, at, :] = lax.select(
                owner_x == outer_x, outer_in[:, :, at, :], resampled[mine_at, :, :, at, :])
            copy = step_copy(1, j)
            copy.start()
            started.append(copy)
        if 0 <= t - 2 < chunks:
            j = t - 2
            at = pl.ds(j * rows, rows)
            step_copy(1, j).wait_recv()
            inner_sel[:, at, :] = lax.select(
                (owner_x == inner_x) | (owner_x == 3 - inner_x),
                inner_in[:, at, :], outer_sel[:, half, at, :])
            copy = step_copy(2, j)
            copy.start()
            started.append(copy)
        if 0 <= t - 3 < chunks:
            j = t - 3
            at = pl.ds(j * rows, rows)
            step_copy(2, j).wait_recv()
            final_own[:, at, :] = lax.select(
                owner_yh == yh, inner_sel[:, at, :], cross_in[:, at, :])
            copy = step_copy(3, j)
            copy.start()
            started.append(copy)
        if t == 1:
            build_band(2)
            build_band(3)
        if 0 <= t - 4 < chunks:
            j = t - 4
            for copy in halo(1, j):
                copy.wait_recv()
            resample(2, j)
            resample(3, j)
            step_copy(3, j).wait_recv()
            looks_of(j)
    for d in range(4):
        at = jnp.where(p0 == d, 0, jnp.where(p1 == d, 1, jnp.where(p2 == d, 2, 3)))
        ml_ref[0, d] = looks[at, 0, :, :, 0:32]
        ml_ref[1, d] = looks[at, 1, :, :, 0:32]
        coh_ref[d] = looks[at, 2, :, :, 0:32]
    for copy in started:
        copy.wait_send()


def on_device(slc, shift_table, phase_table, reference_ids):
    dates_dev, lines = slc.shape[1], slc.shape[2]
    half_lines = lines // 2
    chunks = min(CHUNKS, half_lines // 32)
    rows = half_lines // chunks
    dates, rngs = lax.axis_size("date"), lax.axis_size("rng")
    out_half = half_lines // LOOK_AZ
    vmem = pl.BlockSpec(memory_space=pltpu.VMEM)
    multilook, coherence = pl.pallas_call(
        functools.partial(kernel, dates, rngs, chunks, half_lines),
        out_shape=(
            jax.ShapeDtypeStruct((2, 4, 2, out_half, 32), F32),
            jax.ShapeDtypeStruct((4, 2, out_half, 32), F32),
        ),
        in_specs=[pl.BlockSpec(memory_space=pltpu.SMEM), vmem, vmem, vmem,
                  pl.BlockSpec(memory_space=pl.ANY)],
        out_specs=(vmem, vmem),
        scratch_shapes=[
            pltpu.VMEM((2, 4, 2, half_lines, 512), BF16),
            pltpu.VMEM((2, 4, 2, 2, half_lines, 128), BF16),
            pltpu.VMEM((2, 4, 2, half_lines, 128), BF16),
            pltpu.VMEM((2, 4, 2, 2, half_lines, 128), BF16),
            pltpu.VMEM((2, 4, 2, half_lines, 128), BF16),
            pltpu.VMEM((4, WIN, 512), BF16),
            pltpu.VMEM((4, WIN, 512), BF16),
            pltpu.VMEM((4, 2, 2, half_lines, 512), BF16),
            pltpu.VMEM((2, 2, half_lines, 512), BF16),
            pltpu.VMEM((2, 2, half_lines, 512), BF16),
            pltpu.VMEM((2, half_lines, 512), BF16),
            pltpu.VMEM((2, half_lines, 512), BF16),
            pltpu.VMEM((2, half_lines, 512), BF16),
            pltpu.VMEM((2, half_lines, 512), BF16),
            pltpu.VMEM((2, half_lines, 512), BF16),
            pltpu.VMEM((13 * rows, 128), F32),
            pltpu.VMEM((4, 3, 2, out_half, 128), F32),
            pltpu.SemaphoreType.DMA,
            pltpu.SemaphoreType.DMA((2, chunks, 2, 2)),
            pltpu.SemaphoreType.DMA((2, chunks, 2, 2)),
            pltpu.SemaphoreType.DMA((4, chunks)),
            pltpu.SemaphoreType.DMA((4, chunks)),
        ],
        compiler_params=pltpu.CompilerParams(
            collective_id=0, has_side_effects=True, vmem_limit_bytes=48 * 1024 * 1024),
    )(
        reference_ids,
        shift_table.reshape(4, 1, 512),
        phase_table.reshape(4, 1, 512),
        tap_table(),
        slc.reshape(2, dates_dev, 2, half_lines, 512),
    )
    return multilook.reshape(2, 4, 2 * out_half, 32), coherence.reshape(4, 2 * out_half, 32)


def solution(mesh):
    placed = (P(None, "date", None, "rng"), P("date", "rng"), P("date", "rng"), P())
    return jax.shard_map(
        on_device,
        mesh=mesh,
        in_specs=placed,
        out_specs=(P(None, "date", None, "rng"), P("date", None, "rng")),
        check_vma=False,
    )
```

```python
import functools

import jax
import jax.numpy as jnp
import numpy as np
from jax import lax
from jax.experimental import pallas as pl
from jax.experimental.pallas import tpu as pltpu
from jax.sharding import PartitionSpec as P

TAPS = 8
PHASES = 256
LOOK_AZ = 4
LOOK_RG = 16
CHUNKS = 4
WIN = 768
MESH = pl.DeviceIdType.MESH
BF16 = jnp.bfloat16
F32 = jnp.float32


def tap_table():
    fraction = np.arange(PHASES) / PHASES
    tap_offset = np.arange(TAPS) - (TAPS // 2 - 1)
    t = tap_offset[:, None] - fraction[None, :]
    weight = np.sinc(t) * (0.5 + 0.5 * np.cos(np.pi * t / (TAPS // 2 + 1)))
    weight = jnp.asarray(weight / weight.sum(axis=0, keepdims=True), F32)
    high = weight.astype(BF16)
    low = (weight - high.astype(F32)).astype(BF16)
    return jnp.concatenate([high, low], axis=0)


def half_turn(v):
    return pltpu.roll(v.astype(F32), 64, 1).astype(BF16)


def two_rows(v):
    return v.reshape(-1, v.shape[-1])


def kernel(
    dates, rngs, chunks, half_lines,
    ids_hbm, shift_hbm, phase_hbm, table_hbm, slc_hbm,
    out_ref,
    ids, shift_ref, phase_ref, table_ref,
    own, edge_out, edge_in, band_hi, band_lo,
    resampled, offers, mine_out, merged, cross_in, final,
    lane_sums, power_b, looks, turned,
    own_sem, halo_send, halo_recv, ref_send, ref_recv,
):
    rows = half_lines // chunks
    me_d, me_r = lax.axis_index("date"), lax.axis_index("rng")
    x, yh = me_d // 2, me_d % 2
    outer_x = 3 - x
    inner_x = x + 1 - 2 * (x % 2)
    far_x = 3 - inner_x
    half = x % 2
    left, right = (me_r + rngs - 1) % rngs, (me_r + 1) % rngs
    stack = x // 2
    dev_outer = (outer_x * 2 + yh, me_r)
    dev_inner = (inner_x * 2 + yh, me_r)
    dev_far = (far_x * 2 + yh, me_r)
    dev_cross = (x * 2 + 1 - yh, me_r)
    dev_left, dev_right = (me_d, left), (me_d, right)

    loads = [
        pltpu.make_async_copy(src, dst, own_sem.at[i])
        for i, (src, dst) in enumerate((
            (ids_hbm, ids), (slc_hbm, own), (shift_hbm, shift_ref),
            (phase_hbm, phase_ref), (table_hbm, table_ref)))
    ]
    for copy in loads:
        copy.start()
    barrier = pltpu.get_barrier_semaphore()
    for device in (dev_left, dev_right, dev_outer, dev_far, dev_inner, dev_cross):
        pl.semaphore_signal(barrier, inc=1, device_id=device, device_id_type=MESH)
    loads[0].wait()

    mine = jnp.where(stack == 0, ids[0], ids[1])
    other = jnp.where(stack == 0, ids[1], ids[0])
    slot_m, slot_o = mine % 4, other % 4
    p0 = slot_o
    same = slot_m == slot_o
    p1 = jnp.where(same, (slot_o + 1) % 4, slot_m)
    p2 = jnp.where((p0 != 0) & (p1 != 0), 0, jnp.where((p0 != 1) & (p1 != 1), 1, 2))
    p3 = 6 - p0 - p1 - p2
    order = (p0, p1, p2, p3)
    mine_at = jnp.where(same, 0, 1)
    owner = mine // 4
    owner_x, owner_yh = owner // 2, owner % 2

    lane = lax.broadcasted_iota(jnp.int32, (1, 128), 1)
    started = []

    def stage(i):
        for re_im in range(2):
            edge_out[0, i, re_im] = own[re_im, order[i], :, :, 384:512]
            edge_out[1, i, re_im] = own[re_im, order[i], :, :, 0:128]
        for h in range(2):
            re = own[0, order[i], h, :, 256:384].astype(F32)
            im = own[1, order[i], h, :, 256:384].astype(F32)
            edge_out[0, i, 2, h] = jnp.where(lane < 64, pltpu.roll(re, 64, 1), im).astype(BF16)
            re = own[0, order[i], h, :, 128:256].astype(F32)
            im = own[1, order[i], h, :, 128:256].astype(F32)
            edge_out[1, i, 2, h] = jnp.where(lane < 64, re, pltpu.roll(im, 64, 1)).astype(BF16)

    def halo(i, j):
        at = pl.ds(j * rows, rows)
        return [
            pltpu.make_async_remote_copy(
                src_ref=edge_out.at[side, i, :, :, at, :],
                dst_ref=edge_in.at[side, i, :, :, at, :],
                send_sem=halo_send.at[i, j, side],
                recv_sem=halo_recv.at[i, j, side],
                device_id=device, device_id_type=MESH)
            for side, device in enumerate((dev_right, dev_left))
        ]

    def send_halo(i, j):
        for copy in halo(i, j):
            copy.start()
            started.append(copy)

    def step_copy(step, j):
        at = pl.ds(j * rows, rows)
        src, dst, device = (
            (resampled.at[0, :, 1 - half, at, :], offers.at[0, :, at, :], dev_outer),
            (resampled.at[0, :, half, at, :], offers.at[1, :, at, :], dev_far),
            (mine_out.at[:, at, :], offers.at[2, :, at, :], dev_inner),
            (merged.at[:, at, :], cross_in.at[:, at, :], dev_cross),
            (final.at[:, half, at, :], final.at[:, half, at, :], dev_inner),
        )[step]
        return pltpu.make_async_remote_copy(
            src_ref=src, dst_ref=dst,
            send_sem=ref_send.at[step, j], recv_sem=ref_recv.at[step, j],
            device_id=device, device_id_type=MESH)

    def send_step(step, j):
        copy = step_copy(step, j)
        copy.start()
        started.append(copy)

    def build_band(i):
        phase = phase_ref[pl.ds(order[i], 1), :]
        shift = shift_ref[pl.ds(order[i], 1), :]
        hot = jnp.where(
            lax.broadcasted_iota(jnp.int32, (PHASES, 512), 0) == phase, 1.0, 0.0).astype(BF16)
        taps = jnp.dot(table_ref[...], hot, preferred_element_type=F32)
        column = lax.broadcasted_iota(jnp.int32, (1, 512), 1)
        first = (column & 255) + shift + 253
        block = first >> 3
        place = lax.broadcasted_iota(jnp.int32, (8, 512), 0) - (first & 7)
        parts = []
        for base in (0, 8):
            now = jnp.zeros((8, 512), F32)
            later = jnp.zeros((8, 512), F32)
            for k in range(TAPS):
                tap = taps[base + k:base + k + 1, :]
                now = jnp.where(place == k, tap, now)
                if k > 0:
                    later = jnp.where(place + 8 == k, tap, later)
            parts.append((now, later))
        outside_left = (column < 256) & (me_r == 0)
        outside_right = (column >= 256) & (me_r == rngs - 1)
        regions = (jnp.where(outside_left, -9, block), block, jnp.where(outside_right, -9, block))
        for region, where_at in enumerate(regions):
            spread = jnp.broadcast_to(where_at, (8, 512))

            def fill(t, carry):
                masks = [spread == 2 * t + u for u in (-1, 0, 1)]
                for (now, later), band in zip(parts, (band_hi, band_lo)):
                    low = jnp.where(masks[1], now, jnp.where(masks[0], later, 0.0))
                    up = jnp.where(masks[2], now, jnp.where(masks[1], later, 0.0))
                    band[i, pl.ds(pl.multiple_of(t * 16, 16), 16), :] = (
                        jnp.concatenate([low, up], axis=0).astype(BF16))
                return carry

            lax.fori_loop(region * 16, region * 16 + 16, fill, 0)

    def arrive(i, j):
        for copy in halo(i, j):
            copy.wait_recv()

    def resample(i, j):
        size = half_lines if j is None else rows
        at = pl.ds(0 if j is None else j * rows, size)
        centre = two_rows(own[:, order[i], :, at, :])
        near = [two_rows(edge_in[side, i, 0:2, :, at, :]) for side in range(2)]
        packed = [two_rows(edge_in[side, i, 2, :, at, :]) for side in range(2)]
        before = jnp.concatenate([half_turn(packed[0]), packed[0]], axis=0)
        after = jnp.concatenate([packed[1], half_turn(packed[1])], axis=0)
        windows = (
            jnp.concatenate([before, near[0], centre], axis=1),
            jnp.concatenate([centre, near[1], after], axis=1),
        )
        for n, window in enumerate(windows):
            cols = pl.ds(n * 256, 256)
            total = jnp.dot(window, band_hi[i, :, cols], preferred_element_type=F32)
            total += jnp.dot(window, band_lo[i, :, cols], preferred_element_type=F32)
            resampled[i, :, :, at, cols] = total.astype(BF16).reshape(2, 2, size, 256)

    def offer_other(j):
        arrive(0, j)
        resample(0, j)
        send_step(0, j)
        send_step(1, j)

    def offer_mine(j):
        arrive(1, j)
        resample(1, j)
        at = pl.ds(j * rows, rows)
        mine_out[:, at, :] = resampled[mine_at, :, 1 - half, at, :]
        send_step(2, j)

    def merge(j):
        at = pl.ds(j * rows, rows)
        for step in range(3):
            step_copy(step, j).wait_recv()
        found = lax.select(owner_x == outer_x, offers[0, :, at, :], resampled[mine_at, :, half, at, :])
        found = lax.select(owner_x == far_x, offers[1, :, at, :], found)
        merged[:, at, :] = lax.select(owner_x == inner_x, offers[2, :, at, :], found)
        send_step(3, j)

    def cross(j):
        at = pl.ds(j * rows, rows)
        step_copy(3, j).wait_recv()
        final[:, half, at, :] = lax.select(owner_yh == yh, merged[:, at, :], cross_in[:, at, :])
        send_step(4, j)

    group = lax.broadcasted_iota(jnp.int32, (512, 128), 0) // LOOK_RG
    ones = jnp.where(group == lax.broadcasted_iota(jnp.int32, (512, 128), 1), 1.0, 0.0).astype(BF16)

    def patch_sums(parts):
        count = 2 * rows * len(parts)
        whole = jnp.concatenate(parts, axis=0)
        high = whole.astype(BF16)
        low = (whole - high.astype(F32)).astype(BF16)
        lane_sums[0:count, :] = (
            jnp.dot(high, ones, preferred_element_type=F32)
            + jnp.dot(low, ones, preferred_element_type=F32))
        found = sum(lane_sums[pl.ds(k, count // LOOK_AZ, stride=LOOK_AZ), :] for k in range(LOOK_AZ))
        each = 2 * rows // LOOK_AZ
        return [found[u * each:(u + 1) * each] for u in range(len(parts))]

    def reference_tile(j):
        at = pl.ds(j * rows, rows)
        return [two_rows(final[u, :, at, :]).astype(F32) for u in range(2)]

    def reference_power(j):
        step_copy(4, j).wait_recv()
        b_re, b_im = reference_tile(j)
        power_b[j], = patch_sums([b_re * b_re + b_im * b_im])

    def look(i, j):
        at = pl.ds(j * rows, rows)
        b_re, b_im = reference_tile(j)
        a_re, a_im = (two_rows(resampled[i, u, :, at, :]).astype(F32) for u in range(2))
        s_re, s_im, s_a = patch_sums(
            [a_re * b_re + a_im * b_im, a_im * b_re - a_re * b_im, a_re * a_re + a_im * a_im])
        coherence = jnp.sqrt(s_re * s_re + s_im * s_im) / jnp.sqrt(s_a * power_b[j] + 1e-06)
        out_rows = rows // LOOK_AZ
        to = pl.ds(j * out_rows, out_rows)
        scale = 1.0 / (LOOK_AZ * LOOK_RG)
        for u, v in enumerate((s_re * scale, s_im * scale, coherence)):
            looks[i, u, :, to, :] = v.reshape(2, out_rows, 128)

    def turn(i):
        for u in range(3):
            turned[i, u] = two_rows(looks[i, u]).T[0:32, :]

    loads[1].wait()
    stage(0)
    pl.semaphore_wait(barrier, 6)
    for j in range(chunks):
        send_halo(0, j)
    stage(1)
    for j in range(chunks):
        send_halo(1, j)
    for copy in loads[2:]:
        copy.wait()
    build_band(0)
    build_band(1)
    for j in range(chunks):
        offer_other(j)
    for i in (2, 3):
        stage(i)
        for j in range(chunks):
            send_halo(i, j)
    for j in range(chunks):
        offer_mine(j)
    build_band(2)
    build_band(3)

    def whole(i):
        for j in range(chunks):
            arrive(i, j)
        resample(i, None)

    def looks_at(j, dates_now):
        for i in dates_now:
            look(i, j)

    merge(0)
    merge(1)
    cross(0)
    merge(2)
    whole(2)
    cross(1)
    merge(3)
    reference_power(0)
    looks_at(0, (0, 1, 2))
    cross(2)
    reference_power(1)
    looks_at(1, (0, 1, 2))
    cross(3)
    whole(3)
    reference_power(2)
    looks_at(2, (0, 1, 2, 3))
    looks_at(0, (3,))
    looks_at(1, (3,))
    reference_power(3)
    looks_at(3, (0, 1, 2, 3))
    for i in range(4):
        turn(i)
    for d in range(4):
        at = jnp.where(p0 == d, 0, jnp.where(p1 == d, 1, jnp.where(p2 == d, 2, 3)))
        for u in range(3):
            out_ref[u, d] = turned[at, u]
    for copy in started:
        copy.wait_send()


def hand_out(found_ref, ml_ref, coh_ref, sems):
    ml_ref[...] = found_ref[0:2]
    coh_ref[...] = found_ref[2]


def on_device(slc, shift_table, phase_table, reference_ids):
    dates_dev, lines = slc.shape[1], slc.shape[2]
    half_lines = lines // 2
    chunks = min(CHUNKS, half_lines // 32)
    rows = half_lines // chunks
    dates, rngs = lax.axis_size("date"), lax.axis_size("rng")
    out_half = half_lines // LOOK_AZ
    vmem = pl.BlockSpec(memory_space=pltpu.VMEM)
    found = pl.pallas_call(
        functools.partial(kernel, dates, rngs, chunks, half_lines),
        out_shape=jax.ShapeDtypeStruct((3, 4, 32, 2 * out_half), F32),
        in_specs=[pl.BlockSpec(memory_space=pl.ANY)] * 5,
        out_specs=vmem,
        scratch_shapes=[
            pltpu.SMEM((2,), jnp.int32),
            pltpu.VMEM((4, 512), jnp.int32),
            pltpu.VMEM((4, 512), jnp.int32),
            pltpu.VMEM((2 * TAPS, PHASES), BF16),
            pltpu.VMEM((2, 4, 2, half_lines, 512), BF16),
            pltpu.VMEM((2, 4, 3, 2, half_lines, 128), BF16),
            pltpu.VMEM((2, 4, 3, 2, half_lines, 128), BF16),
            pltpu.VMEM((4, WIN, 512), BF16),
            pltpu.VMEM((4, WIN, 512), BF16),
            pltpu.VMEM((4, 2, 2, half_lines, 512), BF16),
            pltpu.VMEM((3, 2, half_lines, 512), BF16),
            pltpu.VMEM((2, half_lines, 512), BF16),
            pltpu.VMEM((2, half_lines, 512), BF16),
            pltpu.VMEM((2, half_lines, 512), BF16),
            pltpu.VMEM((2, 2, half_lines, 512), BF16),
            pltpu.VMEM((6 * rows, 128), F32),
            pltpu.VMEM((chunks, 2 * rows // LOOK_AZ, 128), F32),
            pltpu.VMEM((4, 3, 2, out_half, 128), F32),
            pltpu.VMEM((4, 3, 32, 2 * out_half), F32),
            pltpu.SemaphoreType.DMA((5,)),
            pltpu.SemaphoreType.DMA((4, chunks, 2)),
            pltpu.SemaphoreType.DMA((4, chunks, 2)),
            pltpu.SemaphoreType.DMA((5, chunks)),
            pltpu.SemaphoreType.DMA((5, chunks)),
        ],
        compiler_params=pltpu.CompilerParams(
            collective_id=0, has_side_effects=True, vmem_limit_bytes=62 * 1024 * 1024),
    )(
        reference_ids,
        shift_table,
        phase_table,
        tap_table(),
        slc.reshape(2, dates_dev, 2, half_lines, 512),
    )
    anywhere = pl.BlockSpec(memory_space=pl.ANY)
    multilook, coherence = pl.pallas_call(
        hand_out,
        out_shape=(
            jax.ShapeDtypeStruct((2, 4, 32, 2 * out_half), F32),
            jax.ShapeDtypeStruct((4, 32, 2 * out_half), F32),
        ),
        in_specs=[vmem],
        out_specs=(vmem, vmem),
        scratch_shapes=[pltpu.SemaphoreType.DMA((2,))],
    )(found)
    return jnp.swapaxes(multilook, 2, 3), jnp.swapaxes(coherence, 1, 2)


def solution(mesh):
    placed = (P(None, "date", None, "rng"), P("date", "rng"), P("date", "rng"), P())
    return jax.shard_map(
        on_device,
        mesh=mesh,
        in_specs=placed,
        out_specs=(P(None, "date", None, "rng"), P("date", None, "rng")),
        check_vma=False,
    )
```

```python
import functools

import jax
import jax.numpy as jnp
import numpy as np
from jax import lax
from jax.experimental import pallas as pl
from jax.experimental.pallas import tpu as pltpu
from jax.sharding import PartitionSpec as P

TAPS = 8
PHASES = 256
LOOK_AZ = 4
LOOK_RG = 16
CHUNKS = (32, 48, 32, 16)
WIN = 768
MESH = pl.DeviceIdType.MESH
BF16 = jnp.bfloat16
F32 = jnp.float32


def tap_table():
    fraction = np.arange(PHASES) / PHASES
    tap_offset = np.arange(TAPS) - (TAPS // 2 - 1)
    t = tap_offset[:, None] - fraction[None, :]
    weight = np.sinc(t) * (0.5 + 0.5 * np.cos(np.pi * t / (TAPS // 2 + 1)))
    weight = jnp.asarray(weight / weight.sum(axis=0, keepdims=True), F32)
    high = weight.astype(BF16)
    low = (weight - high.astype(F32)).astype(BF16)
    return jnp.concatenate([high, low], axis=0)


def half_turn(v):
    return pltpu.roll(v.astype(F32), 64, 1).astype(BF16)


def two_rows(v):
    return v.reshape(-1, v.shape[-1])


def kernel(
    dates, rngs, sizes, blocks, half_lines,
    ids_hbm, shift_hbm, phase_hbm, table_hbm, slc_hbm,
    out_ref,
    ids, shift_ref, phase_ref, table_ref,
    own, edge_out, edge_in, band_hi, band_lo,
    resampled, offers, mine_out, merged, cross_in, final,
    lane_sums, power_b, looks, turned,
    own_sem, halo_send, halo_recv, ref_send, ref_recv,
):
    rows = half_lines // blocks
    chunks = len(sizes)
    starts = [sum(sizes[:j]) for j in range(chunks)]
    pieces = (chunks, chunks, 1, 1)
    me_d, me_r = lax.axis_index("date"), lax.axis_index("rng")
    x, yh = me_d // 2, me_d % 2
    outer_x = 3 - x
    inner_x = x + 1 - 2 * (x % 2)
    far_x = 3 - inner_x
    half = x % 2
    left, right = (me_r + rngs - 1) % rngs, (me_r + 1) % rngs
    stack = x // 2
    dev_outer = (outer_x * 2 + yh, me_r)
    dev_inner = (inner_x * 2 + yh, me_r)
    dev_far = (far_x * 2 + yh, me_r)
    dev_cross = (x * 2 + 1 - yh, me_r)
    dev_left, dev_right = (me_d, left), (me_d, right)

    barrier = pltpu.get_barrier_semaphore()
    for device in (dev_left, dev_right, dev_outer, dev_far, dev_inner, dev_cross):
        pl.semaphore_signal(barrier, inc=1, device_id=device, device_id_type=MESH)
    loads = [
        pltpu.make_async_copy(src, dst, own_sem.at[i])
        for i, (src, dst) in enumerate((
            (ids_hbm, ids), (slc_hbm, own), (shift_hbm, shift_ref),
            (phase_hbm, phase_ref), (table_hbm, table_ref)))
    ]
    for copy in loads:
        copy.start()
    loads[0].wait()

    mine = jnp.where(stack == 0, ids[0], ids[1])
    other = jnp.where(stack == 0, ids[1], ids[0])
    slot_m, slot_o = mine % 4, other % 4
    p0 = slot_o
    same = slot_m == slot_o
    p1 = jnp.where(same, (slot_o + 1) % 4, slot_m)
    p2 = jnp.where((p0 != 0) & (p1 != 0), 0, jnp.where((p0 != 1) & (p1 != 1), 1, 2))
    p3 = 6 - p0 - p1 - p2
    order = (p0, p1, p2, p3)
    mine_at = jnp.where(same, 0, 1)
    owner = mine // 4
    owner_x, owner_yh = owner // 2, owner % 2

    lane = lax.broadcasted_iota(jnp.int32, (1, 128), 1)
    started = []
    landed = list(range(chunks))

    def stage(i):
        for re_im in range(2):
            edge_out[0, i, re_im] = own[re_im, order[i], :, :, 384:512]
            edge_out[1, i, re_im] = own[re_im, order[i], :, :, 0:128]
        for h in range(2):
            re = own[0, order[i], h, :, 256:384].astype(F32)
            im = own[1, order[i], h, :, 256:384].astype(F32)
            edge_out[0, i, 2, h] = jnp.where(lane < 64, pltpu.roll(re, 64, 1), im).astype(BF16)
            re = own[0, order[i], h, :, 128:256].astype(F32)
            im = own[1, order[i], h, :, 128:256].astype(F32)
            edge_out[1, i, 2, h] = jnp.where(lane < 64, re, pltpu.roll(im, 64, 1)).astype(BF16)

    def lines_of(j):
        return pl.ds(starts[j], sizes[j])

    def halo(i, j):
        at = lines_of(j) if i < 2 else pl.ds(0, half_lines)
        return [
            pltpu.make_async_remote_copy(
                src_ref=edge_out.at[side, i, :, :, at, :],
                dst_ref=edge_in.at[side, i, :, :, at, :],
                send_sem=halo_send.at[i, j, side],
                recv_sem=halo_recv.at[i, j, side],
                device_id=device, device_id_type=MESH)
            for side, device in enumerate((dev_right, dev_left))
        ]

    def send_halo(i, j):
        for copy in halo(i, j):
            copy.start()
            started.append(copy)

    def step_copy(step, j):
        at = lines_of(j)
        src, dst, device = (
            (resampled.at[0, :, 1 - half, at, :], offers.at[0, :, at, :], dev_outer),
            (resampled.at[0, :, half, at, :], offers.at[1, :, at, :], dev_far),
            (mine_out.at[:, at, :], offers.at[2, :, at, :], dev_inner),
            (merged.at[:, at, :], cross_in.at[:, at, :], dev_cross),
            (final.at[:, half, at, :], final.at[:, half, at, :], dev_inner),
        )[step]
        return pltpu.make_async_remote_copy(
            src_ref=src, dst_ref=dst,
            send_sem=ref_send.at[step, j], recv_sem=ref_recv.at[step, j],
            device_id=device, device_id_type=MESH)

    def send_step(step, j):
        copy = step_copy(step, j)
        copy.start()
        started.append(copy)

    def build_band(i):
        phase = phase_ref[pl.ds(order[i], 1), :]
        shift = shift_ref[pl.ds(order[i], 1), :]
        hot = jnp.where(
            lax.broadcasted_iota(jnp.int32, (PHASES, 512), 0) == phase, 1.0, 0.0).astype(BF16)
        taps = jnp.dot(table_ref[...], hot, preferred_element_type=F32)
        column = lax.broadcasted_iota(jnp.int32, (1, 512), 1)
        first = (column & 255) + shift + 253
        block = first >> 3
        place = lax.broadcasted_iota(jnp.int32, (8, 512), 0) - (first & 7)
        parts = []
        for base in (0, 8):
            now = jnp.zeros((8, 512), F32)
            later = jnp.zeros((8, 512), F32)
            for k in range(TAPS):
                tap = taps[base + k:base + k + 1, :]
                now = jnp.where(place == k, tap, now)
                if k > 0:
                    later = jnp.where(place + 8 == k, tap, later)
            parts.append((now, later))
        outside_left = (column < 256) & (me_r == 0)
        outside_right = (column >= 256) & (me_r == rngs - 1)
        regions = (jnp.where(outside_left, -9, block), block, jnp.where(outside_right, -9, block))
        for region, where_at in enumerate(regions):
            spread = jnp.broadcast_to(where_at, (8, 512))

            def fill(t, carry):
                masks = [spread == 2 * t + u for u in (-1, 0, 1)]
                for (now, later), band in zip(parts, (band_hi, band_lo)):
                    low = jnp.where(masks[1], now, jnp.where(masks[0], later, 0.0))
                    up = jnp.where(masks[2], now, jnp.where(masks[1], later, 0.0))
                    band[i, pl.ds(pl.multiple_of(t * 16, 16), 16), :] = (
                        jnp.concatenate([low, up], axis=0).astype(BF16))
                return carry

            lax.fori_loop(region * 16, region * 16 + 16, fill, 0)

    def arrive(i, j):
        for copy in halo(i, j):
            copy.wait_recv()

    def resample(i, j):
        size = half_lines if j is None else sizes[j]
        at = pl.ds(0, half_lines) if j is None else lines_of(j)
        centre = two_rows(own[:, order[i], :, at, :])
        near = [two_rows(edge_in[side, i, 0:2, :, at, :]) for side in range(2)]
        packed = [two_rows(edge_in[side, i, 2, :, at, :]) for side in range(2)]
        before = jnp.concatenate([half_turn(packed[0]), packed[0]], axis=0)
        after = jnp.concatenate([packed[1], half_turn(packed[1])], axis=0)
        windows = (
            jnp.concatenate([before, near[0], centre], axis=1),
            jnp.concatenate([centre, near[1], after], axis=1),
        )
        for n, window in enumerate(windows):
            cols = pl.ds(n * 256, 256)
            total = jnp.dot(window, band_hi[i, :, cols], preferred_element_type=F32)
            total += jnp.dot(window, band_lo[i, :, cols], preferred_element_type=F32)
            resampled[i, :, :, at, cols] = total.astype(BF16).reshape(2, 2, size, 256)

    def offer_other(j):
        arrive(0, j)
        resample(0, j)
        send_step(0, j)
        send_step(1, j)

    def offer_mine(j):
        arrive(1, j)
        resample(1, j)
        at = lines_of(j)
        mine_out[:, at, :] = resampled[mine_at, :, 1 - half, at, :]
        send_step(2, j)

    def merge(j):
        at = lines_of(j)
        for step in range(3):
            step_copy(step, j).wait_recv()
        found = lax.select(owner_x == outer_x, offers[0, :, at, :], resampled[mine_at, :, half, at, :])
        found = lax.select(owner_x == far_x, offers[1, :, at, :], found)
        merged[:, at, :] = lax.select(owner_x == inner_x, offers[2, :, at, :], found)
        send_step(3, j)

    def cross(j):
        at = lines_of(j)
        step_copy(3, j).wait_recv()
        final[:, half, at, :] = lax.select(owner_yh == yh, merged[:, at, :], cross_in[:, at, :])
        send_step(4, j)

    group = lax.broadcasted_iota(jnp.int32, (512, 128), 0) // LOOK_RG
    ones = jnp.where(group == lax.broadcasted_iota(jnp.int32, (512, 128), 1), 1.0, 0.0).astype(BF16)

    def patch_sums(parts):
        count = 2 * rows * len(parts)
        whole = jnp.concatenate(parts, axis=0)
        high = whole.astype(BF16)
        low = (whole - high.astype(F32)).astype(BF16)
        lane_sums[0:count, :] = (
            jnp.dot(high, ones, preferred_element_type=F32)
            + jnp.dot(low, ones, preferred_element_type=F32))
        found = sum(lane_sums[pl.ds(k, count // LOOK_AZ, stride=LOOK_AZ), :] for k in range(LOOK_AZ))
        each = 2 * rows // LOOK_AZ
        return [found[u * each:(u + 1) * each] for u in range(len(parts))]

    def reference_tile(j):
        at = pl.ds(j * rows, rows)
        return [two_rows(final[u, :, at, :]).astype(F32) for u in range(2)]

    def reference_power(j):
        while landed and starts[landed[0]] < (j + 1) * rows:
            step_copy(4, landed.pop(0)).wait_recv()
        b_re, b_im = reference_tile(j)
        power_b[j], = patch_sums([b_re * b_re + b_im * b_im])

    def look(i, j):
        at = pl.ds(j * rows, rows)
        b_re, b_im = reference_tile(j)
        a_re, a_im = (two_rows(resampled[i, u, :, at, :]).astype(F32) for u in range(2))
        s_re, s_im, s_a = patch_sums(
            [a_re * b_re + a_im * b_im, a_im * b_re - a_re * b_im, a_re * a_re + a_im * a_im])
        coherence = jnp.sqrt(s_re * s_re + s_im * s_im) / jnp.sqrt(s_a * power_b[j] + 1e-06)
        out_rows = rows // LOOK_AZ
        to = pl.ds(j * out_rows, out_rows)
        scale = 1.0 / (LOOK_AZ * LOOK_RG)
        for u, v in enumerate((s_re * scale, s_im * scale, coherence)):
            looks[i, u, :, to, :] = v.reshape(2, out_rows, 128)

    def turn(i):
        for u in range(3):
            turned[i, u] = two_rows(looks[i, u]).T[0:32, :]

    def whole(i):
        for j in range(pieces[i]):
            arrive(i, j)
        resample(i, None)

    def looks_at(j, dates_now):
        for i in dates_now:
            look(i, j)

    for copy in loads[1:]:
        copy.wait()
    for i in range(4):
        stage(i)
    pl.semaphore_wait(barrier, 6)
    for i in range(4):
        for j in range(pieces[i]):
            send_halo(i, j)
    for i in range(4):
        build_band(i)
    for j in range(chunks):
        offer_other(j)
    for j in range(chunks):
        offer_mine(j)
    merge(0)
    merge(1)
    cross(0)
    merge(2)
    cross(1)
    merge(3)
    whole(2)
    cross(2)
    reference_power(0)
    looks_at(0, (0, 1, 2))
    cross(3)
    whole(3)
    reference_power(1)
    looks_at(1, (0, 1, 2, 3))
    look(3, 0)
    reference_power(2)
    looks_at(2, (0, 1, 2, 3))
    reference_power(3)
    looks_at(3, (0, 1, 2, 3))
    for i in range(4):
        turn(i)
    for d in range(4):
        at = jnp.where(p0 == d, 0, jnp.where(p1 == d, 1, jnp.where(p2 == d, 2, 3)))
        for u in range(3):
            out_ref[u, d] = turned[at, u]
    for copy in started:
        copy.wait_send()


def hand_out(found_ref, ml_ref, coh_ref, sems):
    ml_ref[...] = found_ref[0:2]
    coh_ref[...] = found_ref[2]


def on_device(slc, shift_table, phase_table, reference_ids):
    dates_dev, lines = slc.shape[1], slc.shape[2]
    half_lines = lines // 2
    chunks = len(CHUNKS)
    blocks = half_lines // 32
    rows = half_lines // blocks
    dates, rngs = lax.axis_size("date"), lax.axis_size("rng")
    out_half = half_lines // LOOK_AZ
    vmem = pl.BlockSpec(memory_space=pltpu.VMEM)
    found = pl.pallas_call(
        functools.partial(kernel, dates, rngs, CHUNKS, blocks, half_lines),
        out_shape=jax.ShapeDtypeStruct((3, 4, 32, 2 * out_half), F32),
        in_specs=[pl.BlockSpec(memory_space=pl.ANY)] * 5,
        out_specs=vmem,
        scratch_shapes=[
            pltpu.SMEM((2,), jnp.int32),
            pltpu.VMEM((4, 512), jnp.int32),
            pltpu.VMEM((4, 512), jnp.int32),
            pltpu.VMEM((2 * TAPS, PHASES), BF16),
            pltpu.VMEM((2, 4, 2, half_lines, 512), BF16),
            pltpu.VMEM((2, 4, 3, 2, half_lines, 128), BF16),
            pltpu.VMEM((2, 4, 3, 2, half_lines, 128), BF16),
            pltpu.VMEM((4, WIN, 512), BF16),
            pltpu.VMEM((4, WIN, 512), BF16),
            pltpu.VMEM((4, 2, 2, half_lines, 512), BF16),
            pltpu.VMEM((3, 2, half_lines, 512), BF16),
            pltpu.VMEM((2, half_lines, 512), BF16),
            pltpu.VMEM((2, half_lines, 512), BF16),
            pltpu.VMEM((2, half_lines, 512), BF16),
            pltpu.VMEM((2, 2, half_lines, 512), BF16),
            pltpu.VMEM((6 * rows, 128), F32),
            pltpu.VMEM((blocks, 2 * rows // LOOK_AZ, 128), F32),
            pltpu.VMEM((4, 3, 2, out_half, 128), F32),
            pltpu.VMEM((4, 3, 32, 2 * out_half), F32),
            pltpu.SemaphoreType.DMA((5,)),
            pltpu.SemaphoreType.DMA((4, chunks, 2)),
            pltpu.SemaphoreType.DMA((4, chunks, 2)),
            pltpu.SemaphoreType.DMA((5, chunks)),
            pltpu.SemaphoreType.DMA((5, chunks)),
        ],
        compiler_params=pltpu.CompilerParams(
            collective_id=0, has_side_effects=True, vmem_limit_bytes=62 * 1024 * 1024),
    )(
        reference_ids,
        shift_table,
        phase_table,
        tap_table(),
        slc.reshape(2, dates_dev, 2, half_lines, 512),
    )
    anywhere = pl.BlockSpec(memory_space=pl.ANY)
    multilook, coherence = pl.pallas_call(
        hand_out,
        out_shape=(
            jax.ShapeDtypeStruct((2, 4, 32, 2 * out_half), F32),
            jax.ShapeDtypeStruct((4, 32, 2 * out_half), F32),
        ),
        in_specs=[vmem],
        out_specs=(vmem, vmem),
        scratch_shapes=[pltpu.SemaphoreType.DMA((2,))],
    )(found)
    return jnp.swapaxes(multilook, 2, 3), jnp.swapaxes(coherence, 1, 2)


def solution(mesh):
    placed = (P(None, "date", None, "rng"), P("date", "rng"), P("date", "rng"), P())
    return jax.shard_map(
        on_device,
        mesh=mesh,
        in_specs=placed,
        out_specs=(P(None, "date", None, "rng"), P("date", None, "rng")),
        check_vma=False,
    )
```

```python
import functools

import jax
import jax.numpy as jnp
import numpy as np
from jax import lax
from jax.experimental import pallas as pl
from jax.experimental.pallas import tpu as pltpu
from jax.sharding import PartitionSpec as P

TAPS = 8
PHASES = 256
LOOK_AZ = 4
LOOK_RG = 16
CHUNKS = (32, 48, 32, 16)
WIN = 768
MESH = pl.DeviceIdType.MESH
BF16 = jnp.bfloat16
F32 = jnp.float32


def tap_table():
    fraction = np.arange(PHASES) / PHASES
    tap_offset = np.arange(TAPS) - (TAPS // 2 - 1)
    t = tap_offset[:, None] - fraction[None, :]
    weight = np.sinc(t) * (0.5 + 0.5 * np.cos(np.pi * t / (TAPS // 2 + 1)))
    weight = jnp.asarray(weight / weight.sum(axis=0, keepdims=True), F32)
    high = weight.astype(BF16)
    low = (weight - high.astype(F32)).astype(BF16)
    return jnp.concatenate([high, low], axis=0)


def half_turn(v):
    return pltpu.roll(v.astype(F32), 64, 1).astype(BF16)


def two_rows(v):
    return v.reshape(-1, v.shape[-1])


def kernel(
    dates, rngs, sizes, blocks, half_lines,
    ids_hbm, shift_hbm, phase_hbm, table_hbm, slc_hbm,
    out_ref,
    ids, shift_ref, phase_ref, table_ref,
    own, edge_out, edge_in, band_hi, band_lo,
    resampled, offers, mine_out, merged, cross_in, final,
    lane_sums, power_b, looks, turned,
    own_sem, halo_send, halo_recv, ref_send, ref_recv,
):
    rows = half_lines // blocks
    chunks = len(sizes)
    starts = [sum(sizes[:j]) for j in range(chunks)]
    pieces = (chunks, chunks, 1, 1)
    me_d, me_r = lax.axis_index("date"), lax.axis_index("rng")
    x, yh = me_d // 2, me_d % 2
    outer_x = 3 - x
    inner_x = x + 1 - 2 * (x % 2)
    far_x = 3 - inner_x
    half = x % 2
    left, right = (me_r + rngs - 1) % rngs, (me_r + 1) % rngs
    stack = x // 2
    dev_outer = (outer_x * 2 + yh, me_r)
    dev_inner = (inner_x * 2 + yh, me_r)
    dev_far = (far_x * 2 + yh, me_r)
    dev_cross = (x * 2 + 1 - yh, me_r)
    dev_left, dev_right = (me_d, left), (me_d, right)

    barrier = pltpu.get_barrier_semaphore()
    for device in (dev_left, dev_right, dev_outer, dev_far, dev_inner, dev_cross):
        pl.semaphore_signal(barrier, inc=1, device_id=device, device_id_type=MESH)
    loads = [
        pltpu.make_async_copy(src, dst, own_sem.at[i])
        for i, (src, dst) in enumerate((
            (ids_hbm, ids), (slc_hbm, own), (shift_hbm, shift_ref),
            (phase_hbm, phase_ref), (table_hbm, table_ref)))
    ]
    for copy in loads:
        copy.start()
    loads[0].wait()

    mine = jnp.where(stack == 0, ids[0], ids[1])
    other = jnp.where(stack == 0, ids[1], ids[0])
    slot_m, slot_o = mine % 4, other % 4
    p0 = slot_o
    same = slot_m == slot_o
    p1 = jnp.where(same, (slot_o + 1) % 4, slot_m)
    p2 = jnp.where((p0 != 0) & (p1 != 0), 0, jnp.where((p0 != 1) & (p1 != 1), 1, 2))
    p3 = 6 - p0 - p1 - p2
    order = (p0, p1, p2, p3)
    mine_at = jnp.where(same, 0, 1)
    owner = mine // 4
    owner_x, owner_yh = owner // 2, owner % 2

    lane = lax.broadcasted_iota(jnp.int32, (1, 128), 1)
    started = []
    landed = list(range(chunks))

    def stage(i):
        for re_im in range(2):
            edge_out[0, i, re_im] = own[re_im, order[i], :, :, 384:512]
            edge_out[1, i, re_im] = own[re_im, order[i], :, :, 0:128]
        for h in range(2):
            re = own[0, order[i], h, :, 256:384].astype(F32)
            im = own[1, order[i], h, :, 256:384].astype(F32)
            edge_out[0, i, 2, h] = jnp.where(lane < 64, pltpu.roll(re, 64, 1), im).astype(BF16)
            re = own[0, order[i], h, :, 128:256].astype(F32)
            im = own[1, order[i], h, :, 128:256].astype(F32)
            edge_out[1, i, 2, h] = jnp.where(lane < 64, re, pltpu.roll(im, 64, 1)).astype(BF16)

    def lines_of(j):
        return pl.ds(starts[j], sizes[j])

    def halo(i, j):
        at = lines_of(j) if i < 2 else pl.ds(0, half_lines)
        return [
            pltpu.make_async_remote_copy(
                src_ref=edge_out.at[side, i, :, :, at, :],
                dst_ref=edge_in.at[side, i, :, :, at, :],
                send_sem=halo_send.at[i, j, side],
                recv_sem=halo_recv.at[i, j, side],
                device_id=device, device_id_type=MESH)
            for side, device in enumerate((dev_right, dev_left))
        ]

    def send_halo(i, j):
        for copy in halo(i, j):
            copy.start()
            started.append(copy)

    def step_copy(step, j):
        at = lines_of(j)
        src, dst, device = (
            (resampled.at[0, :, 1 - half, at, :], offers.at[0, :, at, :], dev_outer),
            (resampled.at[0, :, half, at, :], offers.at[1, :, at, :], dev_far),
            (mine_out.at[:, at, :], offers.at[2, :, at, :], dev_inner),
            (merged.at[:, at, :], cross_in.at[:, at, :], dev_cross),
            (final.at[:, half, at, :], final.at[:, half, at, :], dev_inner),
        )[step]
        return pltpu.make_async_remote_copy(
            src_ref=src, dst_ref=dst,
            send_sem=ref_send.at[step, j], recv_sem=ref_recv.at[step, j],
            device_id=device, device_id_type=MESH)

    def send_step(step, j):
        copy = step_copy(step, j)
        copy.start()
        started.append(copy)

    def build_band(i):
        phase = phase_ref[pl.ds(order[i], 1), :]
        shift = shift_ref[pl.ds(order[i], 1), :]
        hot = jnp.where(
            lax.broadcasted_iota(jnp.int32, (PHASES, 512), 0) == phase, 1.0, 0.0).astype(BF16)
        taps = jnp.dot(table_ref[...], hot, preferred_element_type=F32)
        column = lax.broadcasted_iota(jnp.int32, (1, 512), 1)
        first = (column & 255) + shift + 253
        block = first >> 3
        place = lax.broadcasted_iota(jnp.int32, (8, 512), 0) - (first & 7)
        parts = []
        for base in (0, 8):
            now = jnp.zeros((8, 512), F32)
            later = jnp.zeros((8, 512), F32)
            for k in range(TAPS):
                tap = taps[base + k:base + k + 1, :]
                now = jnp.where(place == k, tap, now)
                if k > 0:
                    later = jnp.where(place + 8 == k, tap, later)
            parts.append((now, later))
        outside_left = (column < 256) & (me_r == 0)
        outside_right = (column >= 256) & (me_r == rngs - 1)
        regions = (jnp.where(outside_left, -9, block), block, jnp.where(outside_right, -9, block))
        for region, where_at in enumerate(regions):
            spread = jnp.broadcast_to(where_at, (8, 512))

            def fill(t, carry):
                masks = [spread == 2 * t + u for u in (-1, 0, 1)]
                for (now, later), band in zip(parts, (band_hi, band_lo)):
                    low = jnp.where(masks[1], now, jnp.where(masks[0], later, 0.0))
                    up = jnp.where(masks[2], now, jnp.where(masks[1], later, 0.0))
                    band[i, pl.ds(pl.multiple_of(t * 16, 16), 16), :] = (
                        jnp.concatenate([low, up], axis=0).astype(BF16))
                return carry

            lax.fori_loop(region * 16, region * 16 + 16, fill, 0)

    def arrive(i, j):
        for copy in halo(i, j):
            copy.wait_recv()

    def resample(i, j):
        size = half_lines if j is None else sizes[j]
        at = pl.ds(0, half_lines) if j is None else lines_of(j)
        centre = two_rows(own[:, order[i], :, at, :])
        near = [two_rows(edge_in[side, i, 0:2, :, at, :]) for side in range(2)]
        packed = [two_rows(edge_in[side, i, 2, :, at, :]) for side in range(2)]
        before = jnp.concatenate([half_turn(packed[0]), packed[0]], axis=0)
        after = jnp.concatenate([packed[1], half_turn(packed[1])], axis=0)
        windows = (
            jnp.concatenate([before, near[0], centre], axis=1),
            jnp.concatenate([centre, near[1], after], axis=1),
        )
        for n, window in enumerate(windows):
            cols = pl.ds(n * 256, 256)
            total = jnp.dot(window, band_hi[i, :, cols], preferred_element_type=F32)
            total += jnp.dot(window, band_lo[i, :, cols], preferred_element_type=F32)
            resampled[i, :, :, at, cols] = total.astype(BF16).reshape(2, 2, size, 256)

    def offer_other(j):
        arrive(0, j)
        resample(0, j)
        send_step(0, j)
        send_step(1, j)

    def offer_mine(j):
        arrive(1, j)
        resample(1, j)
        at = lines_of(j)
        mine_out[:, at, :] = resampled[mine_at, :, 1 - half, at, :]
        send_step(2, j)

    def merge(j):
        at = lines_of(j)
        for step in range(3):
            step_copy(step, j).wait_recv()
        found = lax.select(owner_x == outer_x, offers[0, :, at, :], resampled[mine_at, :, half, at, :])
        found = lax.select(owner_x == far_x, offers[1, :, at, :], found)
        merged[:, at, :] = lax.select(owner_x == inner_x, offers[2, :, at, :], found)
        send_step(3, j)

    def cross(j):
        at = lines_of(j)
        step_copy(3, j).wait_recv()
        final[:, half, at, :] = lax.select(owner_yh == yh, merged[:, at, :], cross_in[:, at, :])
        send_step(4, j)

    group = lax.broadcasted_iota(jnp.int32, (512, 128), 0) // LOOK_RG
    ones = jnp.where(group == lax.broadcasted_iota(jnp.int32, (512, 128), 1), 1.0, 0.0).astype(BF16)

    def patch_sums(parts):
        count = 2 * rows * len(parts)
        whole = jnp.concatenate(parts, axis=0)
        high = whole.astype(BF16)
        low = (whole - high.astype(F32)).astype(BF16)
        lane_sums[0:count, :] = (
            jnp.dot(high, ones, preferred_element_type=F32)
            + jnp.dot(low, ones, preferred_element_type=F32))
        found = sum(lane_sums[pl.ds(k, count // LOOK_AZ, stride=LOOK_AZ), :] for k in range(LOOK_AZ))
        each = 2 * rows // LOOK_AZ
        return [found[u * each:(u + 1) * each] for u in range(len(parts))]

    def reference_tile(j):
        at = pl.ds(j * rows, rows)
        return [two_rows(final[u, :, at, :]).astype(F32) for u in range(2)]

    def reference_power(j):
        while landed and starts[landed[0]] < (j + 1) * rows:
            step_copy(4, landed.pop(0)).wait_recv()
        b_re, b_im = reference_tile(j)
        power_b[j], = patch_sums([b_re * b_re + b_im * b_im])

    def look(i, j):
        at = pl.ds(j * rows, rows)
        b_re, b_im = reference_tile(j)
        a_re, a_im = (two_rows(resampled[i, u, :, at, :]).astype(F32) for u in range(2))
        s_re, s_im, s_a = patch_sums(
            [a_re * b_re + a_im * b_im, a_im * b_re - a_re * b_im, a_re * a_re + a_im * a_im])
        coherence = jnp.sqrt(s_re * s_re + s_im * s_im) / jnp.sqrt(s_a * power_b[j] + 1e-06)
        out_rows = rows // LOOK_AZ
        to = pl.ds(j * out_rows, out_rows)
        scale = 1.0 / (LOOK_AZ * LOOK_RG)
        for u, v in enumerate((s_re * scale, s_im * scale, coherence)):
            looks[i, u, :, to, :] = v.reshape(2, out_rows, 128)

    def turn(i):
        for u in range(3):
            turned[i, u] = two_rows(looks[i, u]).T[0:32, :]

    def whole(i):
        for j in range(pieces[i]):
            arrive(i, j)
        resample(i, None)

    def looks_at(j, dates_now):
        for i in dates_now:
            look(i, j)

    loads[1].wait()
    stage(0)
    pl.semaphore_wait(barrier, 6)
    for j in range(chunks):
        send_halo(0, j)
    stage(1)
    for j in range(chunks):
        send_halo(1, j)
    for copy in loads[2:]:
        copy.wait()
    build_band(0)
    build_band(1)
    for i in (2, 3):
        stage(i)
        for j in range(pieces[i]):
            send_halo(i, j)
    build_band(2)
    build_band(3)
    for j in range(chunks):
        offer_other(j)
    for j in range(chunks):
        offer_mine(j)
    merge(0)
    merge(1)
    cross(0)
    merge(2)
    cross(1)
    merge(3)
    whole(2)
    cross(2)
    reference_power(0)
    looks_at(0, (0, 1, 2))
    cross(3)
    whole(3)
    reference_power(1)
    looks_at(1, (0, 1, 2, 3))
    look(3, 0)
    reference_power(2)
    looks_at(2, (0, 1, 2, 3))
    reference_power(3)
    looks_at(3, (0, 1, 2, 3))
    for i in range(4):
        turn(i)
    for d in range(4):
        at = jnp.where(p0 == d, 0, jnp.where(p1 == d, 1, jnp.where(p2 == d, 2, 3)))
        for u in range(3):
            out_ref[u, d] = turned[at, u]
    for copy in started:
        copy.wait_send()


def hand_out(found_ref, ml_ref, coh_ref, sems):
    ml_ref[...] = found_ref[0:2]
    coh_ref[...] = found_ref[2]


def on_device(slc, shift_table, phase_table, reference_ids):
    dates_dev, lines = slc.shape[1], slc.shape[2]
    half_lines = lines // 2
    chunks = len(CHUNKS)
    blocks = half_lines // 32
    rows = half_lines // blocks
    dates, rngs = lax.axis_size("date"), lax.axis_size("rng")
    out_half = half_lines // LOOK_AZ
    vmem = pl.BlockSpec(memory_space=pltpu.VMEM)
    found = pl.pallas_call(
        functools.partial(kernel, dates, rngs, CHUNKS, blocks, half_lines),
        out_shape=jax.ShapeDtypeStruct((3, 4, 32, 2 * out_half), F32),
        in_specs=[pl.BlockSpec(memory_space=pl.ANY)] * 5,
        out_specs=vmem,
        scratch_shapes=[
            pltpu.SMEM((2,), jnp.int32),
            pltpu.VMEM((4, 512), jnp.int32),
            pltpu.VMEM((4, 512), jnp.int32),
            pltpu.VMEM((2 * TAPS, PHASES), BF16),
            pltpu.VMEM((2, 4, 2, half_lines, 512), BF16),
            pltpu.VMEM((2, 4, 3, 2, half_lines, 128), BF16),
            pltpu.VMEM((2, 4, 3, 2, half_lines, 128), BF16),
            pltpu.VMEM((4, WIN, 512), BF16),
            pltpu.VMEM((4, WIN, 512), BF16),
            pltpu.VMEM((4, 2, 2, half_lines, 512), BF16),
            pltpu.VMEM((3, 2, half_lines, 512), BF16),
            pltpu.VMEM((2, half_lines, 512), BF16),
            pltpu.VMEM((2, half_lines, 512), BF16),
            pltpu.VMEM((2, half_lines, 512), BF16),
            pltpu.VMEM((2, 2, half_lines, 512), BF16),
            pltpu.VMEM((6 * rows, 128), F32),
            pltpu.VMEM((blocks, 2 * rows // LOOK_AZ, 128), F32),
            pltpu.VMEM((4, 3, 2, out_half, 128), F32),
            pltpu.VMEM((4, 3, 32, 2 * out_half), F32),
            pltpu.SemaphoreType.DMA((5,)),
            pltpu.SemaphoreType.DMA((4, chunks, 2)),
            pltpu.SemaphoreType.DMA((4, chunks, 2)),
            pltpu.SemaphoreType.DMA((5, chunks)),
            pltpu.SemaphoreType.DMA((5, chunks)),
        ],
        compiler_params=pltpu.CompilerParams(
            collective_id=0, has_side_effects=True, vmem_limit_bytes=62 * 1024 * 1024),
    )(
        reference_ids,
        shift_table,
        phase_table,
        tap_table(),
        slc.reshape(2, dates_dev, 2, half_lines, 512),
    )
    anywhere = pl.BlockSpec(memory_space=pl.ANY)
    multilook, coherence = pl.pallas_call(
        hand_out,
        out_shape=(
            jax.ShapeDtypeStruct((2, 4, 32, 2 * out_half), F32),
            jax.ShapeDtypeStruct((4, 32, 2 * out_half), F32),
        ),
        in_specs=[vmem],
        out_specs=(vmem, vmem),
        scratch_shapes=[pltpu.SemaphoreType.DMA((2,))],
    )(found)
    return jnp.swapaxes(multilook, 2, 3), jnp.swapaxes(coherence, 1, 2)


def solution(mesh):
    placed = (P(None, "date", None, "rng"), P("date", "rng"), P("date", "rng"), P())
    return jax.shard_map(
        on_device,
        mesh=mesh,
        in_specs=placed,
        out_specs=(P(None, "date", None, "rng"), P("date", None, "rng")),
        check_vma=False,
    )
```
